32 devices in a mesh: fsdp: 16 (over z, x, core), col: 2 (over y).
Axes of the slice: x: 2, y: 2, z: 4, core: 2. Of those that a mesh axis runs over, the one named last changes fastest.
Arguments:
- codes: bfloat16 [8192, 26624], P('fsdp', 'col'), may hold values from -96 to 96
- scales: float32 [64, 208], P('fsdp', 'col'), may hold values from 0.01 to 0.1
- factors: float32 [7, 8192, 64], P(None, 'fsdp'), may hold values from -0.225 to 0.225
- upstream: bfloat16 [8192, 26624], P('fsdp', 'col'), may hold values from -0.036621094 to 0.036621094
Outputs:
- factor_grads: float32 [7, 8192, 64], P(None, 'fsdp')
The draws below stay inside these ranges and needn't reach their ends.
All inputs are finite; a program needn't handle non-finite values.
Results may differ from the reference program's by a relative error of at most 0.02.
Values may be sent and summed in bfloat16 or wider, within the bound.
A program may use at most 320 MiB of HBM per device.

```python
import math
import jax
import jax.numpy as jnp
from jax import lax

D = 8192
COLS = 26624
BLOCK = 64
LEVELS = 7
SCALE_BLK = 128


def block_levels(key, extent, shards, low, largest):
    loudness, own = 1.0, jax.random.fold_in(key, 6)
    for dim, blocks in shards:
        draws = jnp.exp(jax.random.uniform(jax.random.fold_in(own, dim), (blocks,), jnp.float32, low / len(shards), largest / len(shards)))
        loudness = loudness * jnp.repeat(draws, extent[dim] // blocks).reshape([-1 if axis == dim else 1 for axis in range(len(extent))])
    return loudness


def scatter_about(stream_key, shape, scale, most, pieces=(), kind=jnp.bfloat16):
    drawn = scale * jax.random.normal(stream_key, shape, jnp.float32)
    if pieces:
        drawn = drawn * block_levels(stream_key, shape, pieces, -0.22, 0.18)
    return jnp.clip(drawn, -most, most).astype(kind)


def setup_inputs(seed: int = 0) -> dict:
    arg_keys = jax.random.split(jax.random.key(seed), 5)
    return {
        "codes": scatter_about(arg_keys[0], (D, COLS), 16.0, 96.0, ((0, 16), (1, 2))),
        "scales": jnp.clip(jnp.exp(math.log(0.1) - 2.3025851 * jax.random.uniform(arg_keys[1], (D // SCALE_BLK, COLS // SCALE_BLK), jnp.float32) ** block_levels(arg_keys[1], (D // SCALE_BLK, COLS // SCALE_BLK), ((0, 16), (1, 2)), -0.2, 0.2)), 0.01, 0.1),
        "factors": scatter_about(arg_keys[2], (LEVELS, D, BLOCK), (0.3 * BLOCK ** -0.5), 0.225, ((1, 16),), jnp.float32),
        "upstream": scatter_about(arg_keys[3], (D, COLS), (COLS ** -0.5), 0.036621094, ((0, 16), (1, 2))),
    }


def rows_eye(first, count, distance):
    half = BLOCK // 2
    rows = first + jnp.arange(count, dtype=jnp.int32)
    pick = ((rows // distance) % 2) * half + rows % half
    return (jnp.arange(BLOCK, dtype=jnp.int32)[None, :] == pick[:, None]).astype(jnp.float32)


def forward_level(mixing, values, distance, count):
    half = BLOCK // 2
    groups = count // (2 * distance)
    parts = distance // half
    wide = values.shape[1]
    mats = mixing.astype(jnp.float32).reshape(groups, 2, parts, half, 2, half)
    vecs = values.astype(jnp.float32).reshape(groups, 2, parts, half, wide)
    out = jnp.einsum("ghqtHs,gHqsc->ghqtc", mats, vecs)
    return out.reshape(count, wide).astype(jnp.bfloat16)


def backward_level(mixing, values, grad, distance, count):
    half = BLOCK // 2
    groups = count // (2 * distance)
    parts = distance // half
    wide = values.shape[1]
    mats = mixing.astype(jnp.float32).reshape(groups, 2, parts, half, 2, half)
    vecs = values.astype(jnp.float32).reshape(groups, 2, parts, half, wide)
    grads = grad.astype(jnp.float32).reshape(groups, 2, parts, half, wide)
    dmix = jnp.einsum("ghqtc,gHqsc->ghqtHs", grads, vecs).reshape(count, BLOCK)
    lower = jnp.einsum("gqtHs,gqtc->gHqsc", mats[:, 0], grads[:, 0]).astype(jnp.bfloat16)
    upper = jnp.einsum("gqtHs,gqtc->gHqsc", mats[:, 1], grads[:, 1]).astype(jnp.bfloat16)
    lower, upper = lax.optimization_barrier((lower, upper))
    back = (lower.astype(jnp.float32) + upper.astype(jnp.float32)).reshape(count, wide).astype(jnp.bfloat16)
    return dmix, back


def reference(codes, scales, factors, upstream):
    half = BLOCK // 2
    mixing = [(rows_eye(0, D, half * 2 ** level) + factors[level]).astype(jnp.bfloat16) for level in range(LEVELS)]
    width = math.gcd(COLS, 1024)
    count = COLS // width

    def one_slab(index, total):
        start = (index * width).astype(jnp.int32)
        piece = lax.dynamic_slice_in_dim(codes, start, width, 1).astype(jnp.float32)
        sstart = (index * (width // SCALE_BLK)).astype(jnp.int32)
        spiece = lax.dynamic_slice_in_dim(scales, sstart, width // SCALE_BLK, 1)
        base = piece.reshape(D // SCALE_BLK, SCALE_BLK, width // SCALE_BLK, SCALE_BLK) * spiece[:, None, :, None]
        values = base.reshape(D, width).astype(jnp.bfloat16)
        saved = []
        for level in range(LEVELS):
            saved.append(values)
            values = forward_level(mixing[level], values, half * 2 ** level, D)
        grad = lax.dynamic_slice_in_dim(upstream, start, width, 1)
        grads = []
        for level in reversed(range(LEVELS)):
            dmix, grad = backward_level(mixing[level], saved[level], grad, half * 2 ** level, D)
            grads.append(dmix)
        grads = grads[::-1]
        return total + jnp.stack(grads)

    start_total = jnp.zeros((LEVELS, D, BLOCK), jnp.float32)
    return lax.fori_loop(0, count, one_slab, start_total)
```

```python
import functools

import jax
import jax.numpy as jnp
from jax import lax
from jax.experimental import pallas as pl
from jax.experimental.pallas import tpu as pltpu
from jax.sharding import PartitionSpec as P

MESH = pl.DeviceIdType.MESH
LANES = 128


def partner(block, axis, bit):
    count = lax.axis_size(axis)
    route = []
    for low in range(count):
        high = low | 1 << bit
        if high != low and high < count:
            route += [(low, high), (high, low)]
    return lax.ppermute(block, axis, route)


def rows_eye(first, count, distance, block):
    half = block // 2
    rows = first + jnp.arange(count, dtype=jnp.int32)
    pick = rows // distance % 2 * half + rows % half
    return (jnp.arange(block, dtype=jnp.int32)[None, :] == pick[:, None]).astype(jnp.float32)


def source_rows(first, count, distance, block):
    half = block // 2
    rows = first + jnp.arange(count, dtype=jnp.int32)
    inputs = jnp.arange(block, dtype=jnp.int32)
    group = rows // (2 * distance)
    part = rows % distance // half
    return (
        2 * distance * group[:, None]
        + distance * (inputs // half)[None, :]
        + half * part[:, None]
        + (inputs % half)[None, :]
    )


def dense_mixing(mixing, columns, width):
    onehot = columns[:, :, None] == jnp.arange(width, dtype=jnp.int32)[None, None, :]
    spread = jnp.where(onehot, mixing[:, :, None], jnp.zeros((), jnp.bfloat16))
    return jnp.sum(spread.astype(jnp.float32), axis=1).astype(jnp.bfloat16)


def left_product(matrix, grad):
    return lax.dot_general(
        matrix, grad, (((0,), (0,)), ((), ())), preferred_element_type=jnp.float32
    )


def local_scores(grad, values, distance, half):
    rows, wide = grad.shape
    groups = rows // (2 * distance)
    parts = distance // half
    grads = grad.reshape(groups, 2, parts, half, wide)
    vecs = values.reshape(groups, 2, parts, half, wide)
    out = jnp.einsum("ghqtc,gHqsc->ghqtHs", grads, vecs, preferred_element_type=jnp.float32)
    return out.reshape(rows, 2 * half)


def half_scores(grad, values, half):
    rows, wide = grad.shape
    grads = grad.reshape(rows // half, half, wide)
    vecs = values.reshape(rows // half, half, wide)
    out = jnp.einsum("qtc,qsc->qts", grads, vecs, preferred_element_type=jnp.float32)
    return out.reshape(rows, half)


def per_device(codes, scales, factors, upstream):
    rows, wide = codes.shape
    levels = factors.shape[0]
    block = factors.shape[2]
    half = block // 2
    scale_side = rows // scales.shape[0]
    index = lax.axis_index("fsdp")
    first = index * rows
    base = codes.astype(jnp.float32).reshape(
        rows // scale_side, scale_side, wide // scale_side, scale_side
    )
    base = (base * scales[:, None, :, None]).reshape(rows, wide).astype(jnp.bfloat16)
    row_ids = first + jnp.arange(rows, dtype=jnp.int32)
    plans = []
    for level in range(levels):
        distance = half * 2**level
        mixing = (rows_eye(first, rows, distance, block) + factors[level]).astype(jnp.bfloat16)
        sources = source_rows(first, rows, distance, block)
        if distance < rows:
            columns = sources - first
            matrix = dense_mixing(mixing, columns, rows)
            plans.append((matrix, None, None, None))
        else:
            stride = distance // rows
            bit = stride.bit_length() - 1
            side = index // stride % 2
            partner_first = first + distance * (1 - 2 * side)
            inside = (sources >= first) & (sources < first + rows)
            columns = jnp.where(inside, sources - first, sources - partner_first + rows)
            matrix = dense_mixing(mixing, columns, 2 * rows)
            plans.append((matrix[:, :rows], matrix[:, rows:], bit, side))
    values = base
    saved = []
    partners = []
    for level in range(levels):
        distance = half * 2**level
        matrix, far_matrix, bit, side = plans[level]
        saved.append(values)
        if distance < rows:
            partners.append(None)
            values = jnp.dot(matrix, values, preferred_element_type=jnp.float32).astype(
                jnp.bfloat16
            )
        else:
            other = partner(values, "fsdp", bit)
            partners.append(other)
            total = jnp.dot(matrix, values, preferred_element_type=jnp.float32)
            total = total + jnp.dot(far_matrix, other, preferred_element_type=jnp.float32)
            values = total.astype(jnp.bfloat16)
    grad = upstream
    results = [None] * levels
    for level in reversed(range(levels)):
        distance = half * 2**level
        matrix, far_matrix, bit, side = plans[level]
        if distance < rows:
            dmix = local_scores(grad, saved[level], distance, half)
            if level > 0:
                upper_rows = (row_ids // distance % 2 == 1)[:, None]
                low_matrix = jnp.where(upper_rows, jnp.zeros((), jnp.bfloat16), matrix)
                high_matrix = jnp.where(upper_rows, matrix, jnp.zeros((), jnp.bfloat16))
                lower = left_product(low_matrix, grad).astype(jnp.bfloat16)
                upper = left_product(high_matrix, grad).astype(jnp.bfloat16)
                grad = (lower.astype(jnp.float32) + upper.astype(jnp.float32)).astype(jnp.bfloat16)
        else:
            own_part = half_scores(grad, saved[level], half)
            far_part = half_scores(grad, partners[level], half)
            first_half = jnp.where(side == 0, own_part, far_part)
            second_half = jnp.where(side == 0, far_part, own_part)
            dmix = jnp.concatenate([first_half, second_half], axis=1)
            near_term = left_product(matrix, grad).astype(jnp.bfloat16)
            got_grad, got_matrix = partner((grad, far_matrix), "fsdp", bit)
            far_term = left_product(got_matrix, got_grad).astype(jnp.bfloat16)
            grad = (near_term.astype(jnp.float32) + far_term.astype(jnp.float32)).astype(
                jnp.bfloat16
            )
        results[level] = dmix
    stacked = jnp.stack(results)
    stacked = lax.psum(stacked, "col")
    return stacked


def flipped(me, mask):
    out, bit = me, 1
    while bit <= mask:
        if mask & bit:
            out = out + bit * (1 - 2 * lax.rem(lax.div(me, bit), 2))
        bit *= 2
    return out


def greet(partners):
    barrier = pltpu.get_barrier_semaphore()
    for device in partners:
        pl.semaphore_signal(barrier, inc=1, device_id=device, device_id_type=MESH)
    pl.semaphore_wait(barrier, len(partners))


def exchange_kernel(
    n, codes_ref, up_ref, mix_ref, scale_ref,
    codes_out, up_out, mix_out, scale_out,
    send_sem, recv_sem, own_sem,
):
    index = lax.axis_index("fsdp")
    me = lax.rem(index, n)
    wide = codes_out.shape[2]
    device = lambda mask: {"fsdp": index - me + flipped(me, mask)}
    greet([device(mask) for mask in range(1, n)])

    def columns(place):
        return pl.ds(pl.multiple_of(place * wide, LANES), wide)

    def send(kind, mask, src, dst, to):
        copy = pltpu.make_async_remote_copy(
            src_ref=src,
            dst_ref=dst,
            send_sem=send_sem.at[kind, mask],
            recv_sem=recv_sem.at[kind, mask],
            device_id=device(to),
            device_id_type=MESH,
        )
        copy.start()
        return copy

    local = [
        pltpu.make_async_copy(mix_ref, mix_out.at[me], own_sem.at[0]),
        pltpu.make_async_copy(scale_ref, scale_out.at[me], own_sem.at[1]),
        pltpu.make_async_copy(codes_ref.at[:, columns(me)], codes_out.at[me], own_sem.at[2]),
        pltpu.make_async_copy(up_ref.at[:, :, columns(me)], up_out.at[:, me], own_sem.at[3]),
    ]
    for copy in local:
        copy.start()
    copies, mixes = [], {}
    for mask in list(range(2, n, 2)) + [1]:
        mixes[mask] = send(0, mask, mix_ref, mix_out.at[me], mask)
    order = sorted(range(1, n), key=lambda mask: -mask)
    for mask in order:
        copies.append(send(1, mask, scale_ref, scale_out.at[me], mask))
    for mask in order:
        src = up_ref.at[:, :, columns(flipped(me, mask))]
        copies.append(send(2, mask, src, up_out.at[:, me], mask))
    for mask in order:
        src = codes_ref.at[:, columns(flipped(me, mask))]
        copies.append(send(3, mask, src, codes_out.at[me], mask))
    for mask in range(2, n, 2):
        mixes[mask].wait()
        block = mix_out.at[flipped(me, mask)]
        copies.append(send(0, mask + 1, block, block, 1))
    mixes[1].wait()
    for copy in copies + local:
        copy.wait()


def exchange(n, codes, upstream, mixing, scales, half):
    rows, cols = codes.shape
    wide = cols // n
    parts = rows // half
    any_space = pl.BlockSpec(memory_space=pl.ANY)
    shapes = (
        jax.ShapeDtypeStruct((n, rows, wide), codes.dtype),
        jax.ShapeDtypeStruct((parts, n, half, wide), upstream.dtype),
        jax.ShapeDtypeStruct((n,) + mixing.shape, mixing.dtype),
        jax.ShapeDtypeStruct((n,) + scales.shape, scales.dtype),
    )
    return pl.pallas_call(
        functools.partial(exchange_kernel, n),
        out_shape=shapes,
        in_specs=[any_space] * 4,
        out_specs=[any_space] * 4,
        scratch_shapes=[
            pltpu.SemaphoreType.DMA((4, n)),
            pltpu.SemaphoreType.DMA((4, n)),
            pltpu.SemaphoreType.DMA((4,)),
        ],
        compiler_params=pltpu.CompilerParams(collective_id=0, has_side_effects=True),
        cost_estimate=pl.CostEstimate(
            flops=0, bytes_accessed=8 * rows * cols, transcendentals=0
        ),
    )(codes, upstream.reshape(parts, half, cols), mixing, scales)


def reduce_kernel(n, part_ref, out_ref, near, held, far, send_sem, recv_sem):
    index = lax.axis_index("fsdp")
    me = lax.rem(index, n)
    device = lambda mask: {"fsdp": index - me + flipped(me, mask)}
    masks = list(range(0, n, 2))
    greet([device(mask) for mask in [1] + masks[1:]])
    rows = out_ref.shape[0]
    step = 64

    def send(slot, src, dst, to):
        copy = pltpu.make_async_remote_copy(
            src_ref=src,
            dst_ref=dst,
            send_sem=send_sem.at[slot],
            recv_sem=recv_sem.at[slot],
            device_id=device(to),
            device_id_type=MESH,
        )
        copy.start()
        return copy

    order = masks[::-1]
    first = {
        mask: send(mask, part_ref.at[flipped(me, mask + 1)], near.at[mask // 2], 1)
        for mask in order
    }
    second = []
    for mask in order:
        first[mask].wait_recv()
        own = flipped(me, mask)

        def add(i, carry, mask=mask, own=own):
            at = pl.ds(pl.multiple_of(i * step, step), step)
            total = part_ref[own, at].astype(jnp.float32) + near[mask // 2, at].astype(
                jnp.float32
            )
            if mask:
                held[mask // 2 - 1, at] = total.astype(held.dtype)
            else:
                out_ref[at] = total
            return carry

        lax.fori_loop(0, rows // step, add, 0)
        if mask:
            second.append(
                send(mask + 1, held.at[mask // 2 - 1], far.at[mask // 2 - 1], mask)
            )
    for copy in second:
        copy.wait_recv()

    def finish(i, carry):
        at = pl.ds(pl.multiple_of(i * step, step), step)
        total = out_ref[at]
        for slot in range(n // 2 - 1):
            total = total + far[slot, at].astype(jnp.float32)
        out_ref[at] = total
        return carry

    lax.fori_loop(0, rows // step, finish, 0)
    for copy in list(first.values()) + second:
        copy.wait_send()


def reduce_parts(n, parts):
    _, rows, wide = parts.shape
    return pl.pallas_call(
        functools.partial(reduce_kernel, n),
        out_shape=jax.ShapeDtypeStruct((rows, wide), jnp.float32),
        in_specs=[pl.BlockSpec(memory_space=pltpu.VMEM)],
        out_specs=pl.BlockSpec(memory_space=pltpu.VMEM),
        scratch_shapes=[
            pltpu.VMEM((n // 2, rows, wide), parts.dtype),
            pltpu.VMEM((n // 2 - 1, rows, wide), parts.dtype),
            pltpu.VMEM((n // 2 - 1, rows, wide), parts.dtype),
            pltpu.SemaphoreType.DMA((n,)),
            pltpu.SemaphoreType.DMA((n,)),
        ],
        compiler_params=pltpu.CompilerParams(
            collective_id=1, has_side_effects=True, vmem_limit_bytes=40 * 2**20
        ),
    )(parts)


def block_mask(count, half, bit, side, dtype):
    rows = lax.broadcasted_iota(jnp.int32, (count, count), 0) // half
    cols = lax.broadcasted_iota(jnp.int32, (count, count), 1) // half
    low = rows // 2**bit % 2
    return (cols == rows + (side - low) * 2**bit).astype(dtype)


def repeat_eye(count, half, dtype):
    place = lax.broadcasted_iota(jnp.int32, (half, count), 1) % half
    return (place == lax.broadcasted_iota(jnp.int32, (half, count), 0)).astype(dtype)


def spread(mix, bit):
    count, half = mix.shape[-2], mix.shape[-1] // 2
    eye = repeat_eye(count, half, jnp.bfloat16)
    wide = [
        jnp.einsum(
            "...ts,sc->...tc", mix[..., side * half : (side + 1) * half], eye,
            preferred_element_type=jnp.float32,
        )
        * block_mask(count, half, bit, side, jnp.float32)
        for side in range(2)
    ]
    return (wide[0] + wide[1]).astype(jnp.bfloat16)


def gather_back(full, bit, half):
    count = full.shape[-1]
    eye = repeat_eye(count, half, jnp.float32)
    return jnp.concatenate(
        [
            jnp.einsum(
                "...tc,sc->...ts", full * block_mask(count, half, bit, side, jnp.float32), eye,
                preferred_element_type=jnp.float32, precision=lax.Precision.HIGHEST,
            )
            for side in range(2)
        ],
        axis=-1,
    )


def product(spec, left, right):
    return jnp.einsum(
        spec, left.astype(jnp.bfloat16), right.astype(jnp.bfloat16),
        preferred_element_type=jnp.float32,
    )


def chain(mats):
    prefix = [None, mats[0]]
    for mat in mats[1:]:
        prefix.append(product("...ij,...jk->...ik", mat, prefix[-1]).astype(jnp.bfloat16))
    return prefix


def level_grads(gram, mats, prefix, half):
    out = [None] * len(mats)
    left = gram
    for bit in reversed(range(len(mats))):
        full = left
        if bit:
            full = product("...ij,...kj->...ik", left, prefix[bit])
            left = product("...ji,...jk->...ik", mats[bit], left)
        out[bit] = gather_back(full, bit, half)
    return out


def per_device_columns(n, codes, scales, factors, upstream):
    rows, cols = codes.shape
    levels, _, block = factors.shape
    half = block // 2
    parts = rows // half
    low = parts.bit_length() - 1
    wide = cols // n
    scale_rows, scale_cols = scales.shape
    side = rows // scale_rows
    index = lax.axis_index("fsdp")
    me = index % n
    first = index * rows
    mixing = jnp.stack(
        [
            (rows_eye(first, rows, half * 2**level, block) + factors[level]).astype(jnp.bfloat16)
            for level in range(levels)
        ]
    )
    packed = mixing.reshape(levels * rows * block // LANES, LANES)
    padded = jnp.pad(scales, ((0, -scale_rows % 8), (0, -scale_cols % LANES)))
    codes_all, up, packed_all, scales_all = exchange(n, codes, upstream, packed, padded, half)
    mix_all = packed_all.reshape(n, levels, rows, block)

    scale = lax.dynamic_slice_in_dim(scales_all[:, :scale_rows], me * (wide // side), wide // side, 2)
    base = codes_all.astype(jnp.float32).reshape(n, scale_rows, side, wide // side, side)
    base = (base * scale[:, :, None, :, None]).astype(jnp.bfloat16).reshape(n, rows, wide)

    inner = [spread(mix_all[:, level], level) for level in range(low)]
    inner_prefix = chain(inner)
    outer_mix = mix_all[:, low:].reshape(n, levels - low, parts, half, block)
    outer_mix = outer_mix.transpose(1, 2, 0, 3, 4).reshape(levels - low, parts, n * half, block)
    outer = [spread(outer_mix[bit], bit) for bit in range(levels - low)]
    outer_prefix = chain(outer)

    up = up.reshape(parts, n * half, wide)
    grad = product("qji,qjc->qic", outer_prefix[-1], up).astype(jnp.bfloat16)
    grad = grad.reshape(parts, n, half, wide).transpose(1, 0, 2, 3).reshape(n, rows, wide)
    values = product("nij,njc->nic", inner_prefix[-1], base).astype(jnp.bfloat16)
    values = values.reshape(n, parts, half, wide).transpose(1, 0, 2, 3)
    values = values.reshape(parts, n * half, wide)
    inner_gram = product("nic,njc->nij", grad, base)
    outer_gram = product("qic,qjc->qij", up, values)
    upper = jnp.concatenate(level_grads(outer_gram, outer, outer_prefix, half), axis=-1)
    upper = upper.reshape(parts, n, half, -1).transpose(1, 0, 2, 3).reshape(n, rows, -1)

    partial = jnp.concatenate([inner_gram, upper], axis=2).astype(jnp.bfloat16)
    total = reduce_parts(n, partial)
    own = [spread(mixing[level], level) for level in range(low)]
    lower = level_grads(total[:, :rows], own, chain(own), half)
    upper = total[:, rows:].reshape(rows, levels - low, block).transpose(1, 0, 2)
    stacked = jnp.concatenate([jnp.stack(lower), upper], axis=0)
    return lax.psum(stacked, "col")


def body(codes, scales, factors, upstream):
    rows, cols = codes.shape
    levels, _, block = factors.shape
    n = block * 2 ** (levels - 1) // rows
    side = rows // scales.shape[0]
    fits = n > 2 and rows % LANES == 0 and cols % (n * LANES) == 0 and cols % (n * side) == 0
    if fits:
        return per_device_columns(n, codes, scales, factors, upstream)
    return per_device(codes, scales, factors, upstream)


def solution(mesh):
    return jax.shard_map(
        body,
        mesh=mesh,
        in_specs=(P("fsdp", "col"), P("fsdp", "col"), P(None, "fsdp", None), P("fsdp", "col")),
        out_specs=P(None, "fsdp", None),
        check_vma=False,
    )
```

```python
import functools

import jax
import jax.numpy as jnp
from jax import lax
from jax.experimental import pallas as pl
from jax.experimental.pallas import tpu as pltpu
from jax.sharding import PartitionSpec as P

MESH = pl.DeviceIdType.MESH
LANES = 128


def partner(block, axis, bit):
    count = lax.axis_size(axis)
    route = []
    for low in range(count):
        high = low | 1 << bit
        if high != low and high < count:
            route += [(low, high), (high, low)]
    return lax.ppermute(block, axis, route)


def rows_eye(first, count, distance, block):
    half = block // 2
    rows = first + jnp.arange(count, dtype=jnp.int32)
    pick = rows // distance % 2 * half + rows % half
    return (jnp.arange(block, dtype=jnp.int32)[None, :] == pick[:, None]).astype(jnp.float32)


def source_rows(first, count, distance, block):
    half = block // 2
    rows = first + jnp.arange(count, dtype=jnp.int32)
    inputs = jnp.arange(block, dtype=jnp.int32)
    group = rows // (2 * distance)
    part = rows % distance // half
    return (
        2 * distance * group[:, None]
        + distance * (inputs // half)[None, :]
        + half * part[:, None]
        + (inputs % half)[None, :]
    )


def dense_mixing(mixing, columns, width):
    onehot = columns[:, :, None] == jnp.arange(width, dtype=jnp.int32)[None, None, :]
    spread = jnp.where(onehot, mixing[:, :, None], jnp.zeros((), jnp.bfloat16))
    return jnp.sum(spread.astype(jnp.float32), axis=1).astype(jnp.bfloat16)


def left_product(matrix, grad):
    return lax.dot_general(
        matrix, grad, (((0,), (0,)), ((), ())), preferred_element_type=jnp.float32
    )


def local_scores(grad, values, distance, half):
    rows, wide = grad.shape
    groups = rows // (2 * distance)
    parts = distance // half
    grads = grad.reshape(groups, 2, parts, half, wide)
    vecs = values.reshape(groups, 2, parts, half, wide)
    out = jnp.einsum("ghqtc,gHqsc->ghqtHs", grads, vecs, preferred_element_type=jnp.float32)
    return out.reshape(rows, 2 * half)


def half_scores(grad, values, half):
    rows, wide = grad.shape
    grads = grad.reshape(rows // half, half, wide)
    vecs = values.reshape(rows // half, half, wide)
    out = jnp.einsum("qtc,qsc->qts", grads, vecs, preferred_element_type=jnp.float32)
    return out.reshape(rows, half)


def per_device(codes, scales, factors, upstream):
    rows, wide = codes.shape
    levels = factors.shape[0]
    block = factors.shape[2]
    half = block // 2
    scale_side = rows // scales.shape[0]
    index = lax.axis_index("fsdp")
    first = index * rows
    base = codes.astype(jnp.float32).reshape(
        rows // scale_side, scale_side, wide // scale_side, scale_side
    )
    base = (base * scales[:, None, :, None]).reshape(rows, wide).astype(jnp.bfloat16)
    row_ids = first + jnp.arange(rows, dtype=jnp.int32)
    plans = []
    for level in range(levels):
        distance = half * 2**level
        mixing = (rows_eye(first, rows, distance, block) + factors[level]).astype(jnp.bfloat16)
        sources = source_rows(first, rows, distance, block)
        if distance < rows:
            columns = sources - first
            matrix = dense_mixing(mixing, columns, rows)
            plans.append((matrix, None, None, None))
        else:
            stride = distance // rows
            bit = stride.bit_length() - 1
            side = index // stride % 2
            partner_first = first + distance * (1 - 2 * side)
            inside = (sources >= first) & (sources < first + rows)
            columns = jnp.where(inside, sources - first, sources - partner_first + rows)
            matrix = dense_mixing(mixing, columns, 2 * rows)
            plans.append((matrix[:, :rows], matrix[:, rows:], bit, side))
    values = base
    saved = []
    partners = []
    for level in range(levels):
        distance = half * 2**level
        matrix, far_matrix, bit, side = plans[level]
        saved.append(values)
        if distance < rows:
            partners.append(None)
            values = jnp.dot(matrix, values, preferred_element_type=jnp.float32).astype(
                jnp.bfloat16
            )
        else:
            other = partner(values, "fsdp", bit)
            partners.append(other)
            total = jnp.dot(matrix, values, preferred_element_type=jnp.float32)
            total = total + jnp.dot(far_matrix, other, preferred_element_type=jnp.float32)
            values = total.astype(jnp.bfloat16)
    grad = upstream
    results = [None] * levels
    for level in reversed(range(levels)):
        distance = half * 2**level
        matrix, far_matrix, bit, side = plans[level]
        if distance < rows:
            dmix = local_scores(grad, saved[level], distance, half)
            if level > 0:
                upper_rows = (row_ids // distance % 2 == 1)[:, None]
                low_matrix = jnp.where(upper_rows, jnp.zeros((), jnp.bfloat16), matrix)
                high_matrix = jnp.where(upper_rows, matrix, jnp.zeros((), jnp.bfloat16))
                lower = left_product(low_matrix, grad).astype(jnp.bfloat16)
                upper = left_product(high_matrix, grad).astype(jnp.bfloat16)
                grad = (lower.astype(jnp.float32) + upper.astype(jnp.float32)).astype(jnp.bfloat16)
        else:
            own_part = half_scores(grad, saved[level], half)
            far_part = half_scores(grad, partners[level], half)
            first_half = jnp.where(side == 0, own_part, far_part)
            second_half = jnp.where(side == 0, far_part, own_part)
            dmix = jnp.concatenate([first_half, second_half], axis=1)
            near_term = left_product(matrix, grad).astype(jnp.bfloat16)
            got_grad, got_matrix = partner((grad, far_matrix), "fsdp", bit)
            far_term = left_product(got_matrix, got_grad).astype(jnp.bfloat16)
            grad = (near_term.astype(jnp.float32) + far_term.astype(jnp.float32)).astype(
                jnp.bfloat16
            )
        results[level] = dmix
    stacked = jnp.stack(results)
    stacked = lax.psum(stacked, "col")
    return stacked


def flipped(me, mask):
    out, bit = me, 1
    while bit <= mask:
        if mask & bit:
            out = out + bit * (1 - 2 * lax.rem(lax.div(me, bit), 2))
        bit *= 2
    return out


def greet(partners):
    barrier = pltpu.get_barrier_semaphore()
    for device in partners:
        pl.semaphore_signal(barrier, inc=1, device_id=device, device_id_type=MESH)
    pl.semaphore_wait(barrier, len(partners))


def exchange_kernel(
    n, codes_ref, up_ref, mix_ref, inner_ref, scale_ref,
    codes_out, up_out, mix_out, inner_out, scale_out,
    send_sem, recv_sem, own_sem,
):
    index = lax.axis_index("fsdp")
    me = lax.rem(index, n)
    wide = codes_out.shape[2]
    device = lambda mask: {"fsdp": index - me + flipped(me, mask)}
    greet([device(mask) for mask in range(1, n)])

    def columns(place):
        return pl.ds(pl.multiple_of(place * wide, LANES), wide)

    def send(kind, mask, src, dst, to):
        copy = pltpu.make_async_remote_copy(
            src_ref=src,
            dst_ref=dst,
            send_sem=send_sem.at[kind, mask],
            recv_sem=recv_sem.at[kind, mask],
            device_id=device(to),
            device_id_type=MESH,
        )
        copy.start()
        return copy

    local = [
        pltpu.make_async_copy(mix_ref, mix_out.at[me], own_sem.at[0]),
        pltpu.make_async_copy(scale_ref, scale_out.at[me], own_sem.at[1]),
        pltpu.make_async_copy(inner_ref, inner_out.at[me], own_sem.at[4]),
        pltpu.make_async_copy(codes_ref.at[:, columns(me)], codes_out.at[me], own_sem.at[2]),
        pltpu.make_async_copy(up_ref.at[:, :, columns(me)], up_out.at[:, me], own_sem.at[3]),
    ]
    for copy in local:
        copy.start()
    copies, mixes = [], {}
    for mask in list(range(2, n, 2)) + [1]:
        mixes[mask] = [
            send(0, mask, mix_ref, mix_out.at[me], mask),
            send(4, mask, inner_ref, inner_out.at[me], mask),
        ]
    order = sorted(range(1, n), key=lambda mask: -mask)
    for mask in order:
        copies.append(send(1, mask, scale_ref, scale_out.at[me], mask))
    for mask in order:
        src = up_ref.at[:, :, columns(flipped(me, mask))]
        copies.append(send(2, mask, src, up_out.at[:, me], mask))
    for mask in order:
        src = codes_ref.at[:, columns(flipped(me, mask))]
        copies.append(send(3, mask, src, codes_out.at[me], mask))
    for mask in range(2, n, 2):
        for kind, out in ((0, mix_out), (4, inner_out)):
            mixes[mask][kind // 4].wait()
            block = out.at[flipped(me, mask)]
            copies.append(send(kind, mask + 1, block, block, 1))
    copies += mixes[1]
    for copy in copies + local:
        copy.wait()


def exchange(n, codes, upstream, mixing, inner, scales, half):
    rows, cols = codes.shape
    wide = cols // n
    parts = rows // half
    any_space = pl.BlockSpec(memory_space=pl.ANY)
    shapes = (
        jax.ShapeDtypeStruct((n, rows, wide), codes.dtype),
        jax.ShapeDtypeStruct((parts, n, half, wide), upstream.dtype),
        jax.ShapeDtypeStruct((n,) + mixing.shape, mixing.dtype),
        jax.ShapeDtypeStruct((n,) + inner.shape, inner.dtype),
        jax.ShapeDtypeStruct((n,) + scales.shape, scales.dtype),
    )
    return pl.pallas_call(
        functools.partial(exchange_kernel, n),
        out_shape=shapes,
        in_specs=[any_space] * 5,
        out_specs=[any_space] * 5,
        scratch_shapes=[
            pltpu.SemaphoreType.DMA((5, n)),
            pltpu.SemaphoreType.DMA((5, n)),
            pltpu.SemaphoreType.DMA((5,)),
        ],
        compiler_params=pltpu.CompilerParams(collective_id=0, has_side_effects=True),
        cost_estimate=pl.CostEstimate(
            flops=0, bytes_accessed=8 * rows * cols, transcendentals=0
        ),
    )(codes, upstream.reshape(parts, half, cols), mixing, inner, scales)


def reduce_kernel(n, pair, part_ref, out_ref, near, held, far, mine, cross, send_sem, recv_sem):
    index = lax.axis_index("fsdp")
    me = lax.rem(index, n)
    device = lambda mask: {"fsdp": index - me + flipped(me, mask)}
    masks = list(range(0, n, 2))
    across = {"col": 1 - lax.axis_index("col")} if pair else None
    greet([device(mask) for mask in [1] + masks[1:]] + ([across] if pair else []))
    rows = out_ref.shape[0]
    step = 32

    def send(slot, src, dst, to):
        copy = pltpu.make_async_remote_copy(
            src_ref=src,
            dst_ref=dst,
            send_sem=send_sem.at[slot],
            recv_sem=recv_sem.at[slot],
            device_id=to,
            device_id_type=MESH,
        )
        copy.start()
        return copy

    order = masks[::-1]
    first = {
        mask: send(mask, part_ref.at[flipped(me, mask + 1)], near.at[mask // 2], device(1))
        for mask in order
    }
    second = []
    for mask in order:
        first[mask].wait_recv()
        own = flipped(me, mask)

        def add(i, carry, mask=mask, own=own):
            at = pl.ds(pl.multiple_of(i * step, step), step)
            total = part_ref[own, at].astype(jnp.float32) + near[mask // 2, at].astype(
                jnp.float32
            )
            if mask:
                held[mask // 2 - 1, at] = total.astype(held.dtype)
            else:
                out_ref[at] = total
            return carry

        lax.fori_loop(0, rows // step, add, 0)
        if mask:
            second.append(
                send(mask + 1, held.at[mask // 2 - 1], far.at[mask // 2 - 1], device(mask))
            )
    for copy in second:
        copy.wait_recv()

    def finish(i, carry):
        at = pl.ds(pl.multiple_of(i * step, step), step)
        total = out_ref[at]
        for slot in range(n // 2 - 1):
            total = total + far[slot, at].astype(jnp.float32)
        if pair:
            mine[at] = total.astype(mine.dtype)
        else:
            out_ref[at] = total
        return carry

    if not pair:
        lax.fori_loop(0, rows // step, finish, 0)
    else:
        pieces = 4
        span = rows // pieces
        third = []
        for piece in range(pieces):
            lax.fori_loop(piece * span // step, (piece + 1) * span // step, finish, 0)
            at = pl.ds(piece * span, span)
            third.append(send(n + piece, mine.at[at], cross.at[at], across))
        for copy in third:
            copy.wait_recv()

        def join(i, carry):
            at = pl.ds(pl.multiple_of(i * step, step), step)
            out_ref[at] = mine[at].astype(jnp.float32) + cross[at].astype(jnp.float32)
            return carry

        lax.fori_loop(0, rows // step, join, 0)
        second += third
    for copy in list(first.values()) + second:
        copy.wait_send()


def reduce_parts(n, pair, parts):
    _, rows, wide = parts.shape
    return pl.pallas_call(
        functools.partial(reduce_kernel, n, pair),
        out_shape=jax.ShapeDtypeStruct((rows, wide), jnp.float32),
        in_specs=[pl.BlockSpec(memory_space=pltpu.VMEM)],
        out_specs=pl.BlockSpec(memory_space=pltpu.VMEM),
        scratch_shapes=[
            pltpu.VMEM((n // 2, rows, wide), parts.dtype),
            pltpu.VMEM((n // 2 - 1, rows, wide), parts.dtype),
            pltpu.VMEM((n // 2 - 1, rows, wide), parts.dtype),
            pltpu.VMEM((rows, wide), parts.dtype),
            pltpu.VMEM((rows, wide), parts.dtype),
            pltpu.SemaphoreType.DMA((n + 4,)),
            pltpu.SemaphoreType.DMA((n + 4,)),
        ],
        compiler_params=pltpu.CompilerParams(
            collective_id=1, has_side_effects=True, vmem_limit_bytes=40 * 2**20
        ),
    )(parts)


def inner_kernel(codes_ref, scale_ref, mat_ref, grad_ref, val_ref, gram_ref, base):
    rows, wide = base.shape
    half = val_ref.shape[2]
    side = rows // scale_ref.shape[1]
    for block in range(rows // side):
        at = slice(block * side, (block + 1) * side)
        scaled = codes_ref[0, at].astype(jnp.float32) * scale_ref[0, block : block + 1]
        base[at] = scaled.astype(base.dtype)
    count = LANES // half
    for block in range(rows // LANES):
        at = slice(block * LANES, (block + 1) * LANES)
        places = slice(block * count, (block + 1) * count)
        out = jnp.dot(mat_ref[0, at], base[...], preferred_element_type=jnp.float32)
        val_ref[places, 0] = out.astype(val_ref.dtype).reshape(count, half, wide)
        grad = grad_ref[places, 0].reshape(LANES, wide)
        gram = lax.dot_general(
            grad, base[...], (((1,), (1,)), ((), ())), preferred_element_type=jnp.float32
        )
        gram_ref[0, at] = gram.astype(gram_ref.dtype)


def inner_pass(codes, scale, mats, grad):
    n, rows, wide = codes.shape
    parts, _, half, _ = grad.shape
    own = lambda shape: pl.BlockSpec((1,) + shape, lambda i: (i, 0, 0))
    spread_out = pl.BlockSpec((parts, 1, half, wide), lambda i: (0, i, 0, 0))
    return pl.pallas_call(
        inner_kernel,
        grid=(n,),
        out_shape=(
            jax.ShapeDtypeStruct(grad.shape, jnp.bfloat16),
            jax.ShapeDtypeStruct((n, rows, rows), jnp.bfloat16),
        ),
        in_specs=[own((rows, wide)), own(scale.shape[1:]), own((rows, rows)), spread_out],
        out_specs=(spread_out, own((rows, rows))),
        scratch_shapes=[pltpu.VMEM((rows, wide), jnp.bfloat16)],
        compiler_params=pltpu.CompilerParams(vmem_limit_bytes=48 * 2**20),
        cost_estimate=pl.CostEstimate(
            flops=4 * n * rows * rows * wide, bytes_accessed=6 * n * rows * wide, transcendentals=0
        ),
    )(codes, scale, mats, grad)


def block_mask(count, half, bit, side, dtype):
    rows = lax.broadcasted_iota(jnp.int32, (count, count), 0) // half
    cols = lax.broadcasted_iota(jnp.int32, (count, count), 1) // half
    low = rows // 2**bit % 2
    return (cols == rows + (side - low) * 2**bit).astype(dtype)


def repeat_eye(count, half, dtype):
    place = lax.broadcasted_iota(jnp.int32, (half, count), 1) % half
    return (place == lax.broadcasted_iota(jnp.int32, (half, count), 0)).astype(dtype)


def spread(mix, bit):
    count, half = mix.shape[-2], mix.shape[-1] // 2
    eye = repeat_eye(count, half, jnp.bfloat16)
    wide = [
        jnp.einsum(
            "...ts,sc->...tc", mix[..., side * half : (side + 1) * half], eye,
            preferred_element_type=jnp.float32,
        )
        * block_mask(count, half, bit, side, jnp.float32)
        for side in range(2)
    ]
    return (wide[0] + wide[1]).astype(jnp.bfloat16)


def gather_back(full, bit, half, kind, precision):
    count = full.shape[-1]
    eye = repeat_eye(count, half, kind)
    full = full.astype(kind)
    return jnp.concatenate(
        [
            jnp.einsum(
                "...tc,sc->...ts", full * block_mask(count, half, bit, side, kind), eye,
                preferred_element_type=jnp.float32, precision=precision,
            )
            for side in range(2)
        ],
        axis=-1,
    )


def product(spec, left, right):
    return jnp.einsum(
        spec, left.astype(jnp.bfloat16), right.astype(jnp.bfloat16),
        preferred_element_type=jnp.float32,
    )


def chain(mats):
    prefix = [None, mats[0]]
    for mat in mats[1:]:
        prefix.append(product("...ij,...jk->...ik", mat, prefix[-1]).astype(jnp.bfloat16))
    return prefix


def level_grads(gram, mats, prefix, half, kind, precision):
    out = [None] * len(mats)
    left = gram
    for bit in reversed(range(len(mats))):
        full = left
        if bit:
            full = product("...ij,...kj->...ik", left, prefix[bit])
            left = product("...ji,...jk->...ik", mats[bit], left)
        out[bit] = gather_back(full, bit, half, kind, precision)
    return out


def per_device_columns(n, codes, scales, factors, upstream):
    rows, cols = codes.shape
    levels, _, block = factors.shape
    half = block // 2
    parts = rows // half
    low = parts.bit_length() - 1
    wide = cols // n
    scale_rows, scale_cols = scales.shape
    side = rows // scale_rows
    index = lax.axis_index("fsdp")
    me = index % n
    first = index * rows
    mixing = jnp.stack(
        [
            (rows_eye(first, rows, half * 2**level, block) + factors[level]).astype(jnp.bfloat16)
            for level in range(levels)
        ]
    )
    own = [spread(mixing[level], level) for level in range(low)]
    own_prefix = chain(own)
    packed = mixing[low:].reshape((levels - low) * rows * block // LANES, LANES)
    padded = jnp.pad(scales, ((0, -scale_rows % 8), (0, -scale_cols % LANES)))
    codes_all, up, packed_all, inner_all, scales_all = exchange(
        n, codes, upstream, packed, own_prefix[-1], padded, half
    )
    scale = lax.dynamic_slice_in_dim(scales_all[:, :scale_rows], me * (wide // side), wide // side, 2)
    scale = jnp.repeat(scale, side, axis=2)

    outer_mix = packed_all.reshape(n, levels - low, parts, half, block)
    outer_mix = outer_mix.transpose(1, 2, 0, 3, 4).reshape(levels - low, parts, n * half, block)
    outer = [spread(outer_mix[bit], bit) for bit in range(levels - low)]
    outer_prefix = chain(outer)

    up = up.reshape(parts, n * half, wide)
    grad = product("qji,qjc->qic", outer_prefix[-1], up).astype(jnp.bfloat16)
    values, inner_gram = inner_pass(
        codes_all, scale, inner_all, grad.reshape(parts, n, half, wide)
    )
    outer_gram = product("qic,qjc->qij", up, values.reshape(parts, n * half, wide))
    upper = level_grads(outer_gram, outer, outer_prefix, half, jnp.bfloat16, None)
    upper = jnp.concatenate(upper, axis=-1).astype(jnp.bfloat16)
    upper = upper.reshape(parts, n, half, -1).transpose(1, 0, 2, 3).reshape(n, rows, -1)

    pair = lax.axis_size("col") == 2
    total = reduce_parts(n, pair, jnp.concatenate([inner_gram, upper], axis=2))
    lower = level_grads(
        total[:, :rows], own, own_prefix, half, jnp.float32, lax.Precision.HIGHEST
    )
    upper = total[:, rows:].reshape(rows, levels - low, block).transpose(1, 0, 2)
    stacked = jnp.concatenate([jnp.stack(lower), upper], axis=0)
    return stacked if pair else lax.psum(stacked, "col")


def body(codes, scales, factors, upstream):
    rows, cols = codes.shape
    levels, _, block = factors.shape
    n = block * 2 ** (levels - 1) // rows
    side = rows // scales.shape[0]
    fits = n > 2 and rows % LANES == 0 and cols % (n * LANES) == 0 and cols % (n * side) == 0
    if fits:
        return per_device_columns(n, codes, scales, factors, upstream)
    return per_device(codes, scales, factors, upstream)


def solution(mesh):
    return jax.shard_map(
        body,
        mesh=mesh,
        in_specs=(P("fsdp", "col"), P("fsdp", "col"), P(None, "fsdp", None), P("fsdp", "col")),
        out_specs=P(None, "fsdp", None),
        check_vma=False,
    )
```

```python
import functools

import jax
import jax.numpy as jnp
from jax import lax
from jax.experimental import pallas as pl
from jax.experimental.pallas import tpu as pltpu
from jax.sharding import PartitionSpec as P

MESH = pl.DeviceIdType.MESH
LANES = 128


def partner(block, axis, bit):
    count = lax.axis_size(axis)
    route = []
    for low in range(count):
        high = low | 1 << bit
        if high != low and high < count:
            route += [(low, high), (high, low)]
    return lax.ppermute(block, axis, route)


def rows_eye(first, count, distance, block):
    half = block // 2
    rows = first + jnp.arange(count, dtype=jnp.int32)
    pick = rows // distance % 2 * half + rows % half
    return (jnp.arange(block, dtype=jnp.int32)[None, :] == pick[:, None]).astype(jnp.float32)


def source_rows(first, count, distance, block):
    half = block // 2
    rows = first + jnp.arange(count, dtype=jnp.int32)
    inputs = jnp.arange(block, dtype=jnp.int32)
    group = rows // (2 * distance)
    part = rows % distance // half
    return (
        2 * distance * group[:, None]
        + distance * (inputs // half)[None, :]
        + half * part[:, None]
        + (inputs % half)[None, :]
    )


def dense_mixing(mixing, columns, width):
    onehot = columns[:, :, None] == jnp.arange(width, dtype=jnp.int32)[None, None, :]
    spread = jnp.where(onehot, mixing[:, :, None], jnp.zeros((), jnp.bfloat16))
    return jnp.sum(spread.astype(jnp.float32), axis=1).astype(jnp.bfloat16)


def left_product(matrix, grad):
    return lax.dot_general(
        matrix, grad, (((0,), (0,)), ((), ())), preferred_element_type=jnp.float32
    )


def local_scores(grad, values, distance, half):
    rows, wide = grad.shape
    groups = rows // (2 * distance)
    parts = distance // half
    grads = grad.reshape(groups, 2, parts, half, wide)
    vecs = values.reshape(groups, 2, parts, half, wide)
    out = jnp.einsum("ghqtc,gHqsc->ghqtHs", grads, vecs, preferred_element_type=jnp.float32)
    return out.reshape(rows, 2 * half)


def half_scores(grad, values, half):
    rows, wide = grad.shape
    grads = grad.reshape(rows // half, half, wide)
    vecs = values.reshape(rows // half, half, wide)
    out = jnp.einsum("qtc,qsc->qts", grads, vecs, preferred_element_type=jnp.float32)
    return out.reshape(rows, half)


def per_device(codes, scales, factors, upstream):
    rows, wide = codes.shape
    levels = factors.shape[0]
    block = factors.shape[2]
    half = block // 2
    scale_side = rows // scales.shape[0]
    index = lax.axis_index("fsdp")
    first = index * rows
    base = codes.astype(jnp.float32).reshape(
        rows // scale_side, scale_side, wide // scale_side, scale_side
    )
    base = (base * scales[:, None, :, None]).reshape(rows, wide).astype(jnp.bfloat16)
    row_ids = first + jnp.arange(rows, dtype=jnp.int32)
    plans = []
    for level in range(levels):
        distance = half * 2**level
        mixing = (rows_eye(first, rows, distance, block) + factors[level]).astype(jnp.bfloat16)
        sources = source_rows(first, rows, distance, block)
        if distance < rows:
            columns = sources - first
            matrix = dense_mixing(mixing, columns, rows)
            plans.append((matrix, None, None, None))
        else:
            stride = distance // rows
            bit = stride.bit_length() - 1
            side = index // stride % 2
            partner_first = first + distance * (1 - 2 * side)
            inside = (sources >= first) & (sources < first + rows)
            columns = jnp.where(inside, sources - first, sources - partner_first + rows)
            matrix = dense_mixing(mixing, columns, 2 * rows)
            plans.append((matrix[:, :rows], matrix[:, rows:], bit, side))
    values = base
    saved = []
    partners = []
    for level in range(levels):
        distance = half * 2**level
        matrix, far_matrix, bit, side = plans[level]
        saved.append(values)
        if distance < rows:
            partners.append(None)
            values = jnp.dot(matrix, values, preferred_element_type=jnp.float32).astype(
                jnp.bfloat16
            )
        else:
            other = partner(values, "fsdp", bit)
            partners.append(other)
            total = jnp.dot(matrix, values, preferred_element_type=jnp.float32)
            total = total + jnp.dot(far_matrix, other, preferred_element_type=jnp.float32)
            values = total.astype(jnp.bfloat16)
    grad = upstream
    results = [None] * levels
    for level in reversed(range(levels)):
        distance = half * 2**level
        matrix, far_matrix, bit, side = plans[level]
        if distance < rows:
            dmix = local_scores(grad, saved[level], distance, half)
            if level > 0:
                upper_rows = (row_ids // distance % 2 == 1)[:, None]
                low_matrix = jnp.where(upper_rows, jnp.zeros((), jnp.bfloat16), matrix)
                high_matrix = jnp.where(upper_rows, matrix, jnp.zeros((), jnp.bfloat16))
                lower = left_product(low_matrix, grad).astype(jnp.bfloat16)
                upper = left_product(high_matrix, grad).astype(jnp.bfloat16)
                grad = (lower.astype(jnp.float32) + upper.astype(jnp.float32)).astype(jnp.bfloat16)
        else:
            own_part = half_scores(grad, saved[level], half)
            far_part = half_scores(grad, partners[level], half)
            first_half = jnp.where(side == 0, own_part, far_part)
            second_half = jnp.where(side == 0, far_part, own_part)
            dmix = jnp.concatenate([first_half, second_half], axis=1)
            near_term = left_product(matrix, grad).astype(jnp.bfloat16)
            got_grad, got_matrix = partner((grad, far_matrix), "fsdp", bit)
            far_term = left_product(got_matrix, got_grad).astype(jnp.bfloat16)
            grad = (near_term.astype(jnp.float32) + far_term.astype(jnp.float32)).astype(
                jnp.bfloat16
            )
        results[level] = dmix
    stacked = jnp.stack(results)
    stacked = lax.psum(stacked, "col")
    return stacked


def flipped(me, mask):
    out, bit = me, 1
    while bit <= mask:
        if mask & bit:
            out = out + bit * (1 - 2 * lax.rem(lax.div(me, bit), 2))
        bit *= 2
    return out


def greet(partners):
    barrier = pltpu.get_barrier_semaphore()
    for device in partners:
        pl.semaphore_signal(barrier, inc=1, device_id=device, device_id_type=MESH)
    pl.semaphore_wait(barrier, len(partners))


def exchange_kernel(
    n, codes_ref, up_ref, mix_ref, inner_ref, scale_ref,
    codes_out, up_out, mix_out, inner_out, scale_out,
    send_sem, recv_sem, own_sem,
):
    index = lax.axis_index("fsdp")
    me = lax.rem(index, n)
    wide = codes_out.shape[2]
    device = lambda mask: {"fsdp": index - me + flipped(me, mask)}
    greet([device(mask) for mask in range(1, n)])

    def columns(place):
        return pl.ds(pl.multiple_of(place * wide, LANES), wide)

    def send(kind, mask, src, dst, to):
        copy = pltpu.make_async_remote_copy(
            src_ref=src,
            dst_ref=dst,
            send_sem=send_sem.at[kind, mask],
            recv_sem=recv_sem.at[kind, mask],
            device_id=device(to),
            device_id_type=MESH,
        )
        copy.start()
        return copy

    local = [
        pltpu.make_async_copy(mix_ref, mix_out.at[me], own_sem.at[0]),
        pltpu.make_async_copy(scale_ref, scale_out.at[me], own_sem.at[1]),
        pltpu.make_async_copy(inner_ref, inner_out.at[me], own_sem.at[4]),
        pltpu.make_async_copy(codes_ref.at[:, columns(me)], codes_out.at[me], own_sem.at[2]),
        pltpu.make_async_copy(up_ref.at[:, :, columns(me)], up_out.at[:, me], own_sem.at[3]),
    ]
    for copy in local:
        copy.start()
    copies, mixes = [], {}
    for mask in list(range(2, n, 2)) + [1]:
        mixes[mask] = [
            send(0, mask, mix_ref, mix_out.at[me], mask),
            send(4, mask, inner_ref, inner_out.at[me], mask),
        ]
    order = sorted(range(1, n), key=lambda mask: -mask)
    for mask in order:
        copies.append(send(1, mask, scale_ref, scale_out.at[me], mask))
    for mask in order:
        src = up_ref.at[:, :, columns(flipped(me, mask))]
        copies.append(send(2, mask, src, up_out.at[:, me], mask))
    for mask in order:
        src = codes_ref.at[:, columns(flipped(me, mask))]
        copies.append(send(3, mask, src, codes_out.at[me], mask))
    for mask in range(2, n, 2):
        for kind, out in ((0, mix_out), (4, inner_out)):
            mixes[mask][kind // 4].wait()
            block = out.at[flipped(me, mask)]
            copies.append(send(kind, mask + 1, block, block, 1))
    copies += mixes[1]
    for copy in copies + local:
        copy.wait()


def exchange(n, codes, upstream, mixing, inner, scales, half):
    rows, cols = codes.shape
    wide = cols // n
    parts = rows // half
    any_space = pl.BlockSpec(memory_space=pl.ANY)
    shapes = (
        jax.ShapeDtypeStruct((n, rows, wide), codes.dtype),
        jax.ShapeDtypeStruct((parts, n, half, wide), upstream.dtype),
        jax.ShapeDtypeStruct((n,) + mixing.shape, mixing.dtype),
        jax.ShapeDtypeStruct((n,) + inner.shape, inner.dtype),
        jax.ShapeDtypeStruct((n,) + scales.shape, scales.dtype),
    )
    return pl.pallas_call(
        functools.partial(exchange_kernel, n),
        out_shape=shapes,
        in_specs=[any_space] * 5,
        out_specs=[any_space] * 5,
        scratch_shapes=[
            pltpu.SemaphoreType.DMA((5, n)),
            pltpu.SemaphoreType.DMA((5, n)),
            pltpu.SemaphoreType.DMA((5,)),
        ],
        compiler_params=pltpu.CompilerParams(collective_id=0, has_side_effects=True),
        cost_estimate=pl.CostEstimate(
            flops=0, bytes_accessed=8 * rows * cols, transcendentals=0
        ),
    )(codes, upstream.reshape(parts, half, cols), mixing, inner, scales)


def reduce_kernel(n, pair, part_ref, out_ref, near, held, far, mine, cross, send_sem, recv_sem):
    index = lax.axis_index("fsdp")
    me = lax.rem(index, n)
    device = lambda mask: {"fsdp": index - me + flipped(me, mask)}
    masks = list(range(0, n, 2))
    across = {"col": 1 - lax.axis_index("col")} if pair else None
    greet([device(mask) for mask in [1] + masks[1:]] + ([across] if pair else []))
    rows = out_ref.shape[0]
    step = 32

    def send(slot, src, dst, to):
        copy = pltpu.make_async_remote_copy(
            src_ref=src,
            dst_ref=dst,
            send_sem=send_sem.at[slot],
            recv_sem=recv_sem.at[slot],
            device_id=to,
            device_id_type=MESH,
        )
        copy.start()
        return copy

    order = masks[::-1]
    first = {
        mask: send(mask, part_ref.at[flipped(me, mask + 1)], near.at[mask // 2], device(1))
        for mask in order
    }
    second = []
    for mask in order:
        first[mask].wait_recv()
        own = flipped(me, mask)

        def add(i, carry, mask=mask, own=own):
            at = pl.ds(pl.multiple_of(i * step, step), step)
            total = part_ref[own, at].astype(jnp.float32) + near[mask // 2, at].astype(
                jnp.float32
            )
            if mask:
                held[mask // 2 - 1, at] = total.astype(held.dtype)
            else:
                out_ref[at] = total
            return carry

        lax.fori_loop(0, rows // step, add, 0)
        if mask:
            second.append(
                send(mask + 1, held.at[mask // 2 - 1], far.at[mask // 2 - 1], device(mask))
            )
    for copy in second:
        copy.wait_recv()

    def finish(i, carry):
        at = pl.ds(pl.multiple_of(i * step, step), step)
        total = out_ref[at]
        for slot in range(n // 2 - 1):
            total = total + far[slot, at].astype(jnp.float32)
        if pair:
            mine[at] = total.astype(mine.dtype)
        else:
            out_ref[at] = total
        return carry

    if not pair:
        lax.fori_loop(0, rows // step, finish, 0)
    else:
        pieces = 4
        span = rows // pieces
        third = []
        for piece in range(pieces):
            lax.fori_loop(piece * span // step, (piece + 1) * span // step, finish, 0)
            at = pl.ds(piece * span, span)
            third.append(send(n + piece, mine.at[at], cross.at[at], across))
        for copy in third:
            copy.wait_recv()

        def join(i, carry):
            at = pl.ds(pl.multiple_of(i * step, step), step)
            out_ref[at] = mine[at].astype(jnp.float32) + cross[at].astype(jnp.float32)
            return carry

        lax.fori_loop(0, rows // step, join, 0)
        second += third
    for copy in list(first.values()) + second:
        copy.wait_send()


def reduce_parts(n, pair, parts):
    _, rows, wide = parts.shape
    return pl.pallas_call(
        functools.partial(reduce_kernel, n, pair),
        out_shape=jax.ShapeDtypeStruct((rows, wide), jnp.float32),
        in_specs=[pl.BlockSpec(memory_space=pltpu.VMEM)],
        out_specs=pl.BlockSpec(memory_space=pltpu.VMEM),
        scratch_shapes=[
            pltpu.VMEM((n // 2, rows, wide), parts.dtype),
            pltpu.VMEM((n // 2 - 1, rows, wide), parts.dtype),
            pltpu.VMEM((n // 2 - 1, rows, wide), parts.dtype),
            pltpu.VMEM((rows, wide), parts.dtype),
            pltpu.VMEM((rows, wide), parts.dtype),
            pltpu.SemaphoreType.DMA((n + 4,)),
            pltpu.SemaphoreType.DMA((n + 4,)),
        ],
        compiler_params=pltpu.CompilerParams(
            collective_id=1, has_side_effects=True, vmem_limit_bytes=40 * 2**20
        ),
    )(parts)


def inner_kernel(codes_ref, scale_ref, mat_ref, grad_ref, val_ref, gram_ref, base):
    rows, wide = base.shape
    half = val_ref.shape[2]
    side = rows // scale_ref.shape[1]
    for block in range(rows // side):
        at = slice(block * side, (block + 1) * side)
        scaled = codes_ref[0, at].astype(jnp.float32) * scale_ref[0, block : block + 1]
        base[at] = scaled.astype(base.dtype)
    count = LANES // half
    for block in range(rows // LANES):
        at = slice(block * LANES, (block + 1) * LANES)
        places = slice(block * count, (block + 1) * count)
        out = jnp.dot(mat_ref[0, at], base[...], preferred_element_type=jnp.float32)
        val_ref[places, 0] = out.astype(val_ref.dtype).reshape(count, half, wide)
        grad = grad_ref[places, 0].reshape(LANES, wide)
        gram = lax.dot_general(
            grad, base[...], (((1,), (1,)), ((), ())), preferred_element_type=jnp.float32
        )
        gram_ref[0, at] = gram.astype(gram_ref.dtype)


def inner_pass(codes, scale, mats, grad):
    n, rows, wide = codes.shape
    parts, _, half, _ = grad.shape
    own = lambda shape: pl.BlockSpec((1,) + shape, lambda i: (i, 0, 0))
    spread_out = pl.BlockSpec((parts, 1, half, wide), lambda i: (0, i, 0, 0))
    return pl.pallas_call(
        inner_kernel,
        grid=(n,),
        out_shape=(
            jax.ShapeDtypeStruct(grad.shape, jnp.bfloat16),
            jax.ShapeDtypeStruct((n, rows, rows), jnp.bfloat16),
        ),
        in_specs=[own((rows, wide)), own(scale.shape[1:]), own((rows, rows)), spread_out],
        out_specs=(spread_out, own((rows, rows))),
        scratch_shapes=[pltpu.VMEM((rows, wide), jnp.bfloat16)],
        compiler_params=pltpu.CompilerParams(vmem_limit_bytes=48 * 2**20),
        cost_estimate=pl.CostEstimate(
            flops=4 * n * rows * rows * wide, bytes_accessed=6 * n * rows * wide, transcendentals=0
        ),
    )(codes, scale, mats, grad)


def block_mask(count, half, bit, side, dtype):
    rows = lax.broadcasted_iota(jnp.int32, (count, count), 0) // half
    cols = lax.broadcasted_iota(jnp.int32, (count, count), 1) // half
    low = rows // 2**bit % 2
    return (cols == rows + (side - low) * 2**bit).astype(dtype)


def repeat_eye(count, half, dtype):
    place = lax.broadcasted_iota(jnp.int32, (half, count), 1) % half
    return (place == lax.broadcasted_iota(jnp.int32, (half, count), 0)).astype(dtype)


def spread(mix, bit):
    count, half = mix.shape[-2], mix.shape[-1] // 2
    eye = repeat_eye(count, half, jnp.bfloat16)
    wide = [
        jnp.einsum(
            "...ts,sc->...tc", mix[..., side * half : (side + 1) * half], eye,
            preferred_element_type=jnp.float32,
        )
        * block_mask(count, half, bit, side, jnp.float32)
        for side in range(2)
    ]
    return (wide[0] + wide[1]).astype(jnp.bfloat16)


def gather_back(fulls, half, kind, precision):
    count, picks = fulls[0].shape[-1], 2 * len(fulls)
    masked = jnp.concatenate(
        [
            full.astype(kind) * block_mask(count, half, bit, side, kind)
            for bit, full in enumerate(fulls)
            for side in range(2)
        ],
        axis=-1,
    )
    shape = (picks * count, picks * half)
    row = lax.broadcasted_iota(jnp.int32, shape, 0)
    col = lax.broadcasted_iota(jnp.int32, shape, 1)
    pick = ((row // count == col // half) & (row % half == col % half)).astype(kind)
    return jnp.einsum(
        "...tc,cs->...ts", masked, pick, preferred_element_type=jnp.float32, precision=precision
    )


def product(spec, left, right):
    return jnp.einsum(
        spec, left.astype(jnp.bfloat16), right.astype(jnp.bfloat16),
        preferred_element_type=jnp.float32,
    )


def chain(mats):
    prefix = [None, mats[0]]
    for mat in mats[1:]:
        prefix.append(product("...ij,...jk->...ik", mat, prefix[-1]).astype(jnp.bfloat16))
    return prefix


def level_grads(gram, mats, prefix, half, kind, precision):
    out = [None] * len(mats)
    left = gram
    for bit in reversed(range(len(mats))):
        full = left
        if bit:
            full = product("...ij,...kj->...ik", left, prefix[bit])
            left = product("...ji,...jk->...ik", mats[bit], left)
        out[bit] = full
    return gather_back(out, half, kind, precision)


def per_device_columns(n, codes, scales, factors, upstream):
    rows, cols = codes.shape
    levels, _, block = factors.shape
    half = block // 2
    parts = rows // half
    low = parts.bit_length() - 1
    wide = cols // n
    scale_rows, scale_cols = scales.shape
    side = rows // scale_rows
    index = lax.axis_index("fsdp")
    me = index % n
    first = index * rows
    mixing = jnp.stack(
        [
            (rows_eye(first, rows, half * 2**level, block) + factors[level]).astype(jnp.bfloat16)
            for level in range(levels)
        ]
    )
    own = [spread(mixing[level], level) for level in range(low)]
    own_prefix = chain(own)
    packed = mixing[low:].reshape((levels - low) * rows * block // LANES, LANES)
    padded = jnp.pad(scales, ((0, -scale_rows % 8), (0, -scale_cols % LANES)))
    codes_all, up, packed_all, inner_all, scales_all = exchange(
        n, codes, upstream, packed, own_prefix[-1], padded, half
    )
    scale = lax.dynamic_slice_in_dim(scales_all[:, :scale_rows], me * (wide // side), wide // side, 2)
    scale = jnp.repeat(scale, side, axis=2)

    outer_mix = packed_all.reshape(n, levels - low, parts, half, block)
    outer_mix = outer_mix.transpose(1, 2, 0, 3, 4).reshape(levels - low, parts, n * half, block)
    outer = [spread(outer_mix[bit], bit) for bit in range(levels - low)]
    outer_prefix = chain(outer)

    up = up.reshape(parts, n * half, wide)
    grad = product("qji,qjc->qic", outer_prefix[-1], up).astype(jnp.bfloat16)
    values, inner_gram = inner_pass(
        codes_all, scale, inner_all, grad.reshape(parts, n, half, wide)
    )
    outer_gram = product("qic,qjc->qij", up, values.reshape(parts, n * half, wide))
    upper = level_grads(outer_gram, outer, outer_prefix, half, jnp.bfloat16, None)
    upper = upper.astype(jnp.bfloat16)
    upper = upper.reshape(parts, n, half, -1).transpose(1, 0, 2, 3).reshape(n, rows, -1)

    pair = lax.axis_size("col") == 2
    total = reduce_parts(n, pair, jnp.concatenate([inner_gram, upper], axis=2))
    lower = level_grads(
        total[:, :rows], own, own_prefix, half, jnp.float32, lax.Precision.HIGHEST
    )
    stacked = jnp.concatenate([lower, total[:, rows:]], axis=1)
    stacked = stacked.reshape(rows, levels, block).transpose(1, 0, 2)
    return stacked if pair else lax.psum(stacked, "col")


def body(codes, scales, factors, upstream):
    rows, cols = codes.shape
    levels, _, block = factors.shape
    n = block * 2 ** (levels - 1) // rows
    side = rows // scales.shape[0]
    fits = n > 2 and rows % LANES == 0 and cols % (n * LANES) == 0 and cols % (n * side) == 0
    if fits:
        return per_device_columns(n, codes, scales, factors, upstream)
    return per_device(codes, scales, factors, upstream)


def solution(mesh):
    return jax.shard_map(
        body,
        mesh=mesh,
        in_specs=(P("fsdp", "col"), P("fsdp", "col"), P(None, "fsdp", None), P("fsdp", "col")),
        out_specs=P(None, "fsdp", None),
        check_vma=False,
    )
```
